32 devices in a mesh: groups: 2 (over y), space: 16 (over z, x, core).
Axes of the slice: x: 2, y: 2, z: 4, core: 2. Of those that a mesh axis runs over, the one named last changes fastest.
Arguments:
- modes: float32 [4, 128, 32, 64], P('groups', None, 'space'), parts along dimension 0, may hold values from -6 to 6
- cell_weight: float32 [32, 128], P('space', 'groups'), parts along dimension 1, may hold values from 0.5 to 2
- seeds: int32 [256], P(('groups', 'space')), parts along dimension 0, may hold values from 0 to 255
- coeff_table: float32 [256, 128], replicated, may hold values from -6 to 6
- force_table: float32 [256, 128], replicated, may hold values from -6 to 6
- visc_table: float32 [256], replicated, may hold values from 0.02 to 0.2
Outputs:
- coefficients: float32 [256, 128], P(('groups', 'space')), parts along dimension 0
The draws below stay inside these ranges and needn't reach their ends.
There are 2 independent parts, one for each index of `groups`. The reference program is written for one: setup_inputs(seed, part) draws one part's arguments, and reference() takes and returns one part's arrays. A program takes and returns all parts, laid end to end along the dimension named above; an argument that names none is the same for every part. Nothing has to cross between parts.
All inputs are finite; a program needn't handle non-finite values.
Results may differ from the reference program's by a relative error of at most 0.00013.
Values sent between devices are 32-bit elements; how exact they have to be, the bound alone decides.
No kernel may reach another device: no remote copies, remote signals or barrier semaphores. Data moves between devices by JAX's collectives and lax.ppermute only.
A program may use at most 64 MiB of HBM per device.

```python
import math
import jax
import jax.numpy as jnp
from jax import lax

M = 128
NY = 64
PARAMS = 256
STEPS = 2
NX = 32
TRAJ = 128


def plant(drawn, rng, low, top_value):
    longest = drawn.shape.index(max(drawn.shape))
    spots = []
    for shift in (0, 1):
        where = [jax.random.randint(jax.random.fold_in(rng, axis), (), 0, length) for axis, length in enumerate(drawn.shape)]
        where[longest] = (where[longest] + shift) % drawn.shape[longest]
        spots.append(tuple(where))
    return drawn.at[spots[0]].set(low).at[spots[1]].set(top_value)


def block_scale(stream_key, extent, shards, smallest, top_value):
    factor_of = 1.0
    for axis_at, parts in shards:
        steps = jax.random.uniform(jax.random.fold_in(jax.random.fold_in(stream_key, 6), axis_at), (parts,), jnp.float32, smallest / len(shards), top_value / len(shards))
        factor_of = factor_of * jnp.repeat(jnp.exp(steps), extent[axis_at] // parts).reshape((-1,) + (1,) * (len(extent) - 1 - axis_at))
    return factor_of


def scatter_about(stream_key, extent, deviation, reach, shards=(), held_as=jnp.bfloat16):
    values = deviation * jax.random.normal(stream_key, extent, jnp.float32)
    if shards:
        values = values * block_scale(stream_key, extent, shards, -0.22, 0.18)
    return jnp.clip(values, -reach, reach).astype(held_as)


def setup_inputs(seed: int = 0, part: int = 0) -> dict:
    streams_of = jax.random.split(jax.random.key(seed), 7)
    part_keys = jax.random.split(jax.random.fold_in(streams_of[6], part), 7)
    return {
        "modes": scatter_about(part_keys[0], (2, M, NX, NY), 1.0, 6.0, ((2, 16),), jnp.float32),
        "cell_weight": jnp.clip(jnp.exp(math.log(2.0) - 1.3862944 * jax.random.uniform(part_keys[1], (NX, NY), jnp.float32) ** block_scale(part_keys[1], (NX, NY), ((0, 16),), -0.2, 0.2)), 0.5, 2.0),
        "seeds": plant(jax.random.randint(part_keys[2], (TRAJ,), 0, PARAMS), jax.random.fold_in(part_keys[2], 1), 0, PARAMS - 1).astype(jnp.int32),
        "coeff_table": scatter_about(streams_of[3], (PARAMS, M), 1.0, 6.0, (), jnp.float32),
        "force_table": scatter_about(streams_of[4], (PARAMS, M), 1.0, 6.0, (), jnp.float32),
        "visc_table": jnp.clip(jnp.exp(jax.random.uniform(streams_of[5], (PARAMS,), jnp.float32, math.log(0.02), math.log(0.2))), 0.02, 0.2),
    }


TIME_STEP = 0.5


def slopes_of(modes):
    along = (jnp.roll(modes, 2, 2) - 8.0 * jnp.roll(modes, 1, 2) + 8.0 * jnp.roll(modes, -1, 2) - jnp.roll(modes, -2, 2)) / 12.0
    across = (jnp.roll(modes, 2, 3) - 8.0 * jnp.roll(modes, 1, 3) + 8.0 * jnp.roll(modes, -1, 3) - jnp.roll(modes, -2, 3)) / 12.0
    return jnp.stack([along, across])


def reference(modes, cell_weight, seeds, coeff_table, force_table, visc_table):
    cell_count = NX * NY
    slopes = slopes_of(modes).reshape(2, 2, M, cell_count)
    velocity = modes.reshape(2, M, cell_count)
    cell_scale = cell_weight.reshape(cell_count) / cell_count
    weighted = velocity * cell_scale[None, None, :]
    diffusion = jnp.einsum("taic,tajc->ij", slopes * cell_scale[None, None, None, :], slopes, precision=lax.Precision.HIGHEST)
    block_size = 4

    def project(block_index):
        weighted_block = lax.dynamic_slice_in_dim(weighted, block_index * block_size, block_size, 1)
        advected = jnp.sum(weighted_block[None, :, :, None, :] * slopes[:, :, None, :, :], axis=1)
        return jnp.einsum("tjc,tikc->ijk", velocity, advected, precision=lax.Precision.HIGHEST)

    tensor = lax.map(project, jnp.arange(M // block_size, dtype=jnp.int32)).reshape(M * M, M)
    selector = (seeds[:, None] == jnp.arange(PARAMS, dtype=jnp.int32)[None, :]).astype(jnp.float32)
    coeffs = jnp.dot(selector, coeff_table, precision=lax.Precision.HIGHEST)
    forcing = jnp.dot(selector, force_table, precision=lax.Precision.HIGHEST)
    viscosity = jnp.dot(selector, visc_table, precision=lax.Precision.HIGHEST)
    for repeat in range(STEPS):
        paired = jnp.dot(coeffs, tensor.T, precision=lax.Precision.HIGHEST).reshape(TRAJ, M, M)
        quadratic = jnp.sum(paired * coeffs[:, None, :], axis=2)
        linear = jnp.dot(coeffs, diffusion, precision=lax.Precision.HIGHEST)
        coeffs = coeffs + TIME_STEP * (forcing - viscosity[:, None] * linear - quadratic)
    return coeffs
```

```python
import functools

import jax
import jax.numpy as jnp
from jax import lax
from jax.experimental import pallas as pl
from jax.experimental.pallas import tpu as pltpu
from jax.sharding import PartitionSpec as P

STEPS = 2


TIME_STEP = 0.5
SPARE_ROWS = 8


def pack_kernel(modes_ref, weight_ref, chunk_ref):
    components, mode_count, layers, across = modes_ref.shape
    for a in range(components):
        for layer in range(layers):
            chunk_ref[a * mode_count : (a + 1) * mode_count, layer * across : (layer + 1) * across] = modes_ref[
                a, :, layer, :
            ]
    rows = components * mode_count
    for layer in range(layers):
        chunk_ref[rows : rows + SPARE_ROWS, layer * across : (layer + 1) * across] = jnp.broadcast_to(
            weight_ref[layer : layer + 1, :], (SPARE_ROWS, across)
        )


def pack(modes, cell_weight):
    components, mode_count, layers, across = modes.shape
    return pl.pallas_call(
        pack_kernel,
        out_shape=jax.ShapeDtypeStruct((components * mode_count + SPARE_ROWS, layers * across), jnp.float32),
        name="pack",
    )(modes, cell_weight)


def exchange(array, mask):
    devices = lax.axis_size("space")
    return lax.ppermute(array, "space", [(i, i ^ mask) for i in range(devices)])


def spread(array, masks):
    held = {0: array}
    for mask in masks:
        for place in list(held):
            held[place ^ mask] = exchange(held[place], mask)
    return held


def gather(chunk):
    devices = lax.axis_size("space")
    if devices < 16 or devices & (devices - 1):
        everyone = lax.all_gather(chunk, "space")
        return [everyone[j] for j in range(devices)], False
    near = devices // 4
    far = devices // 2 + near
    side = []
    while 2 << len(side) < near:
        side.append(2 << len(side))
    opposite = exchange(chunk, far)
    held = spread(chunk, side + [near])
    for place, array in spread(opposite, [near] + side).items():
        held[far ^ place] = array
    for place in list(held):
        held[place ^ 1] = exchange(held[place], 1)
    return [held[j] for j in range(devices)], True


def halves(array):
    high = array.astype(jnp.bfloat16)
    low = (array - high.astype(jnp.float32)).astype(jnp.bfloat16)
    return high, low


def step_kernel(
    layers, across, me_ref, seeds_ref, visc_ref, coeff_ref, force_ref, *refs
):
    *chunk_refs, out_ref, mode_ref, weight_ref, start_ref, force_rows_ref = refs
    devices = len(chunk_refs)
    own, mode_count = out_ref.shape
    components = mode_ref.shape[0]
    lanes = layers * across
    total_cells = devices * lanes

    me = me_ref[0]
    for j, chunk_ref in enumerate(chunk_refs):
        place = jnp.bitwise_xor(me, j)
        columns = pl.ds(pl.multiple_of(place * lanes, lanes), lanes)
        for a in range(components):
            high, low = halves(chunk_ref[a * mode_count : (a + 1) * mode_count, :])
            mode_ref[a, 0:mode_count, columns] = high
            mode_ref[a, mode_count : 2 * mode_count, columns] = low
        rows = components * mode_count
        weight_ref[:, columns] = chunk_ref[rows : rows + SPARE_ROWS, :] / total_cells

    row_id = lax.broadcasted_iota(jnp.int32, (own, lanes), 0)
    visc = jnp.zeros((own, lanes), jnp.float32)
    for n in range(own):
        seed = seeds_ref[n]
        start_ref[n : n + 1, :] = coeff_ref[pl.ds(seed, 1), :]
        force_rows_ref[n : n + 1, :] = force_ref[pl.ds(seed, 1), :]
        visc = jnp.where(row_id == n, visc_ref[seed], visc)
    coeffs = start_ref[...]
    forcing = force_rows_ref[...]

    lane = lax.broadcasted_iota(jnp.int32, (own, lanes), 1)
    y = lane % across

    def along(field, shift):
        whole, part = divmod(shift, layers)
        if part == 0:
            return [field[(p + whole) % devices] for p in range(devices)]
        rolled = [pltpu.roll(f, (lanes - part * across) % lanes, 1) for f in field]
        inside = lane < (layers - part) * across
        return [
            jnp.where(inside, rolled[(p + whole) % devices], rolled[(p + whole + 1) % devices]) for p in range(devices)
        ]

    def across_by(f, shift):
        plain = pltpu.roll(f, -shift % lanes, 1)
        if shift > 0:
            return jnp.where(y < across - shift, plain, pltpu.roll(f, (across - shift) % lanes, 1))
        return jnp.where(y >= -shift, plain, pltpu.roll(f, (lanes - across - shift) % lanes, 1))

    def slope(m2, m1, p1, p2):
        return (m2 - 8.0 * m1 + 8.0 * p1 - p2) / 12.0

    def slope_along(field):
        shifted = [along(field, s) for s in (-2, -1, 1, 2)]
        return [slope(*(s[p] for s in shifted)) for p in range(devices)]

    def slope_across(field):
        return [slope(*(across_by(f, s) for s in (-2, -1, 1, 2))) for f in field]

    weight = [weight_ref[0:1, p * lanes : (p + 1) * lanes] for p in range(devices)]

    for repeat in range(STEPS):
        high, low = halves(coeffs)
        left = jnp.concatenate(
            [jnp.concatenate([high, high], axis=1), jnp.concatenate([low, low], axis=1)], axis=0
        )
        flow = []
        for a in range(components):
            both = jnp.dot(left, mode_ref[a], preferred_element_type=jnp.float32)
            both = both[:own] + both[own:]
            flow.append([both[:, p * lanes : (p + 1) * lanes] for p in range(devices)])
        change = jnp.zeros((own, mode_count), jnp.float32)
        for a in range(components):
            x_slope = slope_along(flow[a])
            y_slope = slope_across(flow[a])
            x_flux = [weight[p] * x_slope[p] for p in range(devices)]
            y_flux = [weight[p] * y_slope[p] for p in range(devices)]
            x_spread = slope_along(x_flux)
            y_spread = slope_across(y_flux)
            source = jnp.concatenate(
                [
                    flow[0][p] * x_flux[p] + flow[1][p] * y_flux[p] - visc * (x_spread[p] + y_spread[p])
                    for p in range(devices)
                ],
                axis=1,
            )
            high, low = halves(source)
            right = lax.dot_general(
                jnp.concatenate([high, low], axis=0),
                mode_ref[a],
                (((1,), (1,)), ((), ())),
                preferred_element_type=jnp.float32,
            )
            right = right[:own] + right[own:]
            change = change + right[:, :mode_count] + right[:, mode_count:]
        coeffs = coeffs + TIME_STEP * (forcing - change)
    out_ref[...] = coeffs


def shards(modes, cell_weight, seeds, coeff_table, force_table, visc_table):
    components, mode_count, layers, across = modes.shape
    own = seeds.shape[0]
    chunks, by_offset = gather(pack(modes, cell_weight))
    me = jnp.full((1,), lax.axis_index("space") if by_offset else 0, jnp.int32)
    smem = pl.BlockSpec(memory_space=pltpu.SMEM)
    vmem = pl.BlockSpec(memory_space=pltpu.VMEM)
    cells = len(chunks) * layers * across
    return pl.pallas_call(
        functools.partial(step_kernel, layers, across),
        out_shape=jax.ShapeDtypeStruct((own, mode_count), jnp.float32),
        in_specs=[smem] * 3 + [vmem] * (2 + len(chunks)),
        out_specs=vmem,
        scratch_shapes=[
            pltpu.VMEM((components, 2 * mode_count, cells), jnp.bfloat16),
            pltpu.VMEM((SPARE_ROWS, cells), jnp.float32),
            pltpu.VMEM((own, mode_count), jnp.float32),
            pltpu.VMEM((own, mode_count), jnp.float32),
        ],
        compiler_params=pltpu.CompilerParams(vmem_limit_bytes=56 * 1024 * 1024),
        name="steps",
    )(me, seeds, visc_table, coeff_table, force_table, *chunks)


def solution(mesh):
    placed = (
        P("groups", None, "space", None),
        P("space", "groups"),
        P(("groups", "space")),
        P(),
        P(),
        P(),
    )
    return jax.shard_map(
        shards, mesh=mesh, in_specs=placed, out_specs=P(("groups", "space"), None), check_vma=False
    )
```

```python
import functools

import jax
import jax.numpy as jnp
from jax import lax
from jax.experimental import pallas as pl
from jax.experimental.pallas import tpu as pltpu
from jax.sharding import PartitionSpec as P

STEPS = 2


TIME_STEP = 0.5
SPARE_ROWS = 8


def pack_kernel(modes_ref, weight_ref, chunk_ref):
    rows = modes_ref.shape[0]
    layers, across = weight_ref.shape
    chunk_ref[0:rows, :] = modes_ref[...]
    for layer in range(layers):
        chunk_ref[rows : rows + SPARE_ROWS, layer * across : (layer + 1) * across] = jnp.broadcast_to(
            weight_ref[layer : layer + 1, :], (SPARE_ROWS, across)
        )


def pack(modes, cell_weight):
    rows, mode_count = modes.shape
    return pl.pallas_call(
        pack_kernel,
        out_shape=jax.ShapeDtypeStruct((rows + SPARE_ROWS, mode_count), jnp.float32),
        in_specs=[pl.BlockSpec(memory_space=pltpu.VMEM)] * 2,
        out_specs=pl.BlockSpec(memory_space=pltpu.VMEM),
        compiler_params=pltpu.CompilerParams(vmem_limit_bytes=2 * 1024 * 1024),
        name="pack",
    )(modes, cell_weight)


def exchange(held, even_mask, odd_mask):
    array, even, odd = held
    devices = lax.axis_size("space")
    pairs = [(i, i ^ (odd_mask if i & 1 else even_mask)) for i in range(devices)]
    array = lax.ppermute(array, "space", pairs)
    if even_mask & 1:
        even, odd = odd, even
    return array, even ^ even_mask, odd ^ odd_mask


def gather(modes, cell_weight, first_needed):
    components, mode_count, layers, across = modes.shape
    rows = modes.transpose(0, 2, 3, 1).reshape(components * layers * across, mode_count)
    devices = lax.axis_size("space")
    if devices < 16 or devices & (devices - 1):
        everyone = lax.all_gather(pack(rows, cell_weight), "space")
        return [(everyone[j], j, j) for j in range(devices)], False
    far = devices // 2
    near = far // 2
    side = near // 2
    far_rows, even, odd = exchange((rows, 0, 0), far, far)
    far_weight = exchange((cell_weight, 0, 0), far, far)[0]
    own = (pack(rows, cell_weight), 0, 0)
    far_rows, *_ = lax.optimization_barrier((far_rows, *first_needed))
    opposite = (pack(far_rows, far_weight), even, odd)
    held = []
    for start in (own, opposite):
        first = exchange(start, near, side)
        second = exchange(start, side, near)
        held += [start, first, second, exchange(first, side, near)]
    mask = side // 2
    while mask:
        held += [exchange(one, mask, mask) for one in held]
        mask //= 2
    return held, True


def halves(array):
    high = array.astype(jnp.bfloat16)
    low = (array - high.astype(jnp.float32)).astype(jnp.bfloat16)
    return high, low


def select_kernel(seeds_ref, visc_table_ref, coeff_table_ref, force_table_ref, coeff_ref, force_ref, visc_ref):
    own, mode_count = coeff_ref.shape
    row_id = lax.broadcasted_iota(jnp.int32, (own, mode_count), 0)
    visc = jnp.zeros((own, mode_count), jnp.float32)
    for n in range(own):
        seed = seeds_ref[n]
        coeff_ref[n : n + 1, :] = coeff_table_ref[pl.ds(seed, 1), :]
        force_ref[n : n + 1, :] = force_table_ref[pl.ds(seed, 1), :]
        visc = jnp.where(row_id == n, visc_table_ref[seed], visc)
    visc_ref[...] = visc


def select(seeds, coeff_table, force_table, visc_table):
    smem = pl.BlockSpec(memory_space=pltpu.SMEM)
    vmem = pl.BlockSpec(memory_space=pltpu.VMEM)
    rows = jax.ShapeDtypeStruct((seeds.shape[0], coeff_table.shape[1]), jnp.float32)
    return pl.pallas_call(
        select_kernel,
        out_shape=(rows, rows, rows),
        in_specs=[smem, smem, vmem, vmem],
        out_specs=(vmem, vmem, vmem),
        compiler_params=pltpu.CompilerParams(vmem_limit_bytes=2 * 1024 * 1024),
        name="select",
    )(seeds, visc_table, coeff_table, force_table)


def step_kernel(offsets, across, me_ref, coeff_ref, force_ref, visc_ref, *refs):
    *chunk_refs, out_ref, mode_ref, weight_ref = refs
    own, mode_count = out_ref.shape
    components = mode_ref.shape[0]
    devices, lanes = weight_ref.shape
    layers = lanes // across
    total_cells = devices * lanes

    me = me_ref[0, 0]
    odd = me % 2 == 1

    for (even_offset, odd_offset), chunk_ref in zip(offsets, chunk_refs):
        place = jnp.bitwise_xor(me, jnp.where(odd, odd_offset, even_offset))
        rows = pl.ds(pl.multiple_of(place * lanes, lanes), lanes)
        for a in range(components):
            high, low = halves(chunk_ref[a * lanes : (a + 1) * lanes, :])
            mode_ref[a, rows, 0:mode_count] = high
            mode_ref[a, rows, mode_count : 2 * mode_count] = low
        weight_ref[pl.ds(place, 1), :] = chunk_ref[components * lanes : components * lanes + 1, :] / total_cells

    visc = visc_ref[...]
    coeffs = coeff_ref[...]
    forcing = force_ref[...]

    lane = lax.broadcasted_iota(jnp.int32, (own, lanes), 1)
    y = lane % across

    def along(field, shift):
        whole, part = divmod(shift, layers)
        if part == 0:
            return [field[(p + whole) % devices] for p in range(devices)]
        rolled = [pltpu.roll(f, (lanes - part * across) % lanes, 1) for f in field]
        inside = lane < (layers - part) * across
        return [
            jnp.where(inside, rolled[(p + whole) % devices], rolled[(p + whole + 1) % devices]) for p in range(devices)
        ]

    def across_by(f, shift):
        plain = pltpu.roll(f, -shift % lanes, 1)
        if shift > 0:
            return jnp.where(y < across - shift, plain, pltpu.roll(f, (across - shift) % lanes, 1))
        return jnp.where(y >= -shift, plain, pltpu.roll(f, (lanes - across - shift) % lanes, 1))

    def slope(m2, m1, p1, p2):
        return (m2 - 8.0 * m1 + 8.0 * p1 - p2) / 12.0

    def slope_along(field):
        shifted = [along(field, s) for s in (-2, -1, 1, 2)]
        return [slope(*(s[p] for s in shifted)) for p in range(devices)]

    def slope_across(field):
        return [slope(*(across_by(f, s) for s in (-2, -1, 1, 2))) for f in field]

    weight = [weight_ref[p : p + 1, :] for p in range(devices)]

    for repeat in range(STEPS):
        high, low = halves(coeffs)
        left = jnp.concatenate(
            [jnp.concatenate([high, high], axis=1), jnp.concatenate([low, low], axis=1)], axis=0
        )
        flow = []
        for a in range(components):
            both = lax.dot_general(
                left, mode_ref[a], (((1,), (1,)), ((), ())), preferred_element_type=jnp.float32
            )
            both = both[:own] + both[own:]
            flow.append([both[:, p * lanes : (p + 1) * lanes] for p in range(devices)])
        change = jnp.zeros((own, mode_count), jnp.float32)
        for a in range(components):
            x_slope = slope_along(flow[a])
            y_slope = slope_across(flow[a])
            x_flux = [weight[p] * x_slope[p] for p in range(devices)]
            y_flux = [weight[p] * y_slope[p] for p in range(devices)]
            x_spread = slope_along(x_flux)
            y_spread = slope_across(y_flux)
            source = jnp.concatenate(
                [
                    flow[0][p] * x_flux[p] + flow[1][p] * y_flux[p] - visc * (x_spread[p] + y_spread[p])
                    for p in range(devices)
                ],
                axis=1,
            )
            high, low = halves(source)
            right = jnp.dot(
                jnp.concatenate([high, low], axis=0), mode_ref[a], preferred_element_type=jnp.float32
            )
            right = right[:own] + right[own:]
            change = change + right[:, :mode_count] + right[:, mode_count:]
        coeffs = coeffs + TIME_STEP * (forcing - change)
    out_ref[...] = coeffs


def shards(modes, cell_weight, seeds, coeff_table, force_table, visc_table):
    components, mode_count, layers, across = modes.shape
    own = seeds.shape[0]
    lanes = layers * across
    devices = lax.axis_size("space")
    rows = select(seeds, coeff_table, force_table, visc_table)
    chunks, by_offset = gather(modes, cell_weight, rows)
    position = lax.axis_index("space") if by_offset else 0
    me = jnp.full((1, 128), position, jnp.int32)
    vmem = pl.BlockSpec(memory_space=pltpu.VMEM)
    operands = (me, *rows, *(one[0] for one in chunks))
    gathered = 4 * components * devices * lanes * mode_count
    return pl.pallas_call(
        functools.partial(
            step_kernel,
            [one[1:] for one in chunks],
            across,
        ),
        out_shape=jax.ShapeDtypeStruct((own, mode_count), jnp.float32),
        in_specs=[vmem] * len(operands),
        out_specs=vmem,
        scratch_shapes=[
            pltpu.VMEM((components, devices * lanes, 2 * mode_count), jnp.bfloat16),
            pltpu.VMEM((devices, lanes), jnp.float32),
        ],
        compiler_params=pltpu.CompilerParams(vmem_limit_bytes=2 * gathered + 8 * 1024 * 1024),
        name="steps",
    )(*operands)


def solution(mesh):
    placed = (
        P("groups", None, "space", None),
        P("space", "groups"),
        P(("groups", "space")),
        P(),
        P(),
        P(),
    )
    return jax.shard_map(
        shards, mesh=mesh, in_specs=placed, out_specs=P(("groups", "space"), None), check_vma=False
    )
```

```python
import functools

import jax
import jax.numpy as jnp
from jax import lax
from jax.experimental import pallas as pl
from jax.experimental.pallas import tpu as pltpu
from jax.sharding import PartitionSpec as P

STEPS = 2


TIME_STEP = 0.5
SPARE_ROWS = 8
SLOPE_SCALE = 12.0
COMPONENTS = 2


def lay_kernel(weight_ref, row_ref):
    layers, across = weight_ref.shape
    for layer in range(layers):
        row_ref[:, layer * across : (layer + 1) * across] = jnp.broadcast_to(
            weight_ref[layer : layer + 1, :], (SPARE_ROWS, across)
        )


def lay(cell_weight):
    layers, across = cell_weight.shape
    return pl.pallas_call(
        lay_kernel,
        out_shape=jax.ShapeDtypeStruct((SPARE_ROWS, layers * across), jnp.float32),
        in_specs=[pl.BlockSpec(memory_space=pltpu.VMEM)],
        out_specs=pl.BlockSpec(memory_space=pltpu.VMEM),
        compiler_params=pltpu.CompilerParams(vmem_limit_bytes=1024 * 1024),
        name="lay",
    )(cell_weight)


def pack_kernel(modes_ref, row_ref, chunk_ref):
    rows = modes_ref.shape[0]
    chunk_ref[0:rows, :] = modes_ref[...]
    chunk_ref[rows : rows + SPARE_ROWS, :] = row_ref[...]


def pack(modes, weight_rows):
    rows, mode_count = modes.shape
    return pl.pallas_call(
        pack_kernel,
        out_shape=jax.ShapeDtypeStruct((rows + SPARE_ROWS, mode_count), jnp.float32),
        in_specs=[pl.BlockSpec(memory_space=pltpu.VMEM)] * 2,
        out_specs=pl.BlockSpec(memory_space=pltpu.VMEM),
        compiler_params=pltpu.CompilerParams(vmem_limit_bytes=2 * 1024 * 1024),
        name="pack",
    )(modes, weight_rows)


def exchange(held, even_mask, odd_mask):
    array, even, odd = held
    devices = lax.axis_size("space")
    pairs = [(i, i ^ (odd_mask if i & 1 else even_mask)) for i in range(devices)]
    array = lax.ppermute(array, "space", pairs)
    if even_mask & 1:
        even, odd = odd, even
    return array, even ^ even_mask, odd ^ odd_mask


def gather(modes, cell_weight, first_needed):
    components, mode_count, layers, across = modes.shape
    rows = modes.transpose(0, 2, 3, 1).reshape(components * layers * across, mode_count)
    devices = lax.axis_size("space")
    if devices < 16 or devices & (devices - 1):
        everyone = lax.all_gather(pack(rows, lay(cell_weight)), "space")
        return [[(everyone[j], j, j) for j in range(devices)]], False
    near = devices // 4
    side = near // 2
    far = devices // 2 + near
    far_rows, even, odd = exchange((rows, 0, 0), far, far)
    far_weight = exchange((cell_weight, 0, 0), far, far)[0]
    own = (pack(rows, lay(cell_weight)), 0, 0)
    far_rows, *_ = lax.optimization_barrier((far_rows, *first_needed))
    opposite = (pack(far_rows, lay(far_weight)), even, odd)
    held = []
    for start in (own, opposite):
        first = exchange(start, near, side)
        second = exchange(start, side, near)
        held += [start, first, second, exchange(first, side, near)]
    order = [0,0,0,1,0,0,0,2]
    mask = side // 2
    while mask:
        held += [exchange(one, mask, mask) for one in held]
        order += order
        mask //= 2
    groups = [[one for one, at in zip(held, order) if at == wanted] for wanted in range(3)]
    return groups, True


def halves(array):
    high = array.astype(jnp.bfloat16)
    low = (array - high.astype(jnp.float32)).astype(jnp.bfloat16)
    return high, low


def select_kernel(seeds_ref, visc_table_ref, coeff_table_ref, force_table_ref, coeff_ref, force_ref, visc_ref):
    own, mode_count = coeff_ref.shape
    row_id = lax.broadcasted_iota(jnp.int32, (own, mode_count), 0)
    visc = jnp.zeros((own, mode_count), jnp.float32)
    for n in range(own):
        seed = seeds_ref[n]
        coeff_ref[n : n + 1, :] = coeff_table_ref[pl.ds(seed, 1), :]
        force_ref[n : n + 1, :] = force_table_ref[pl.ds(seed, 1), :]
        visc = jnp.where(row_id == n, visc_table_ref[seed], visc)
    visc_ref[...] = visc


def select(seeds, coeff_table, force_table, visc_table):
    smem = pl.BlockSpec(memory_space=pltpu.SMEM)
    vmem = pl.BlockSpec(memory_space=pltpu.VMEM)
    rows = jax.ShapeDtypeStruct((seeds.shape[0], coeff_table.shape[1]), jnp.float32)
    return pl.pallas_call(
        select_kernel,
        out_shape=(rows, rows, rows),
        in_specs=[smem, smem, vmem, vmem],
        out_specs=(vmem, vmem, vmem),
        compiler_params=pltpu.CompilerParams(vmem_limit_bytes=2 * 1024 * 1024),
        name="select",
    )(seeds, visc_table, coeff_table, force_table)


def placing(me, offsets):
    odd = me % 2 == 1
    return [jnp.bitwise_xor(me, jnp.where(odd, odd_offset, even_offset)) for even_offset, odd_offset in offsets]


def take_in(coeffs, places, chunk_refs, flow_ref, weight_ref, mode_refs):
    own, mode_count = coeffs.shape
    components, devices, _, lanes = flow_ref.shape
    total_cells = devices * lanes
    high, low = halves(coeffs)
    left = jnp.concatenate([jnp.concatenate([high, high], axis=1), jnp.concatenate([low, low], axis=1)], axis=0)
    for place, chunk_ref in zip(places, chunk_refs):
        rows = pl.ds(pl.multiple_of(place * lanes, lanes), lanes)
        for a in range(components):
            split = jnp.concatenate(halves(chunk_ref[a * lanes : (a + 1) * lanes, :]), axis=1)
            mode_refs[a][rows, :] = split
            both = lax.dot_general(left, split, (((1,), (1,)), ((), ())), preferred_element_type=jnp.float32)
            flow_ref[a, place] = both[:own] + both[own:]
        last = components * lanes
        weight_ref[pl.ds(place, 1), :] = chunk_ref[last : last + 1, :] / (SLOPE_SCALE * total_cells)


def take_in_kernel(offsets, me_ref, coeff_ref, *refs):
    chunk_refs = refs[: len(offsets)]
    kept = refs[-2 - COMPONENTS :]
    take_in(coeff_ref[...], placing(me_ref[0, 0], offsets), chunk_refs, kept[0], kept[1], kept[2:])


def state_of(components, devices, own, lanes, mode_count):
    return (
        jax.ShapeDtypeStruct((components, devices, own, lanes), jnp.float32),
        jax.ShapeDtypeStruct((devices, lanes), jnp.float32),
        *[jax.ShapeDtypeStruct((devices * lanes, 2 * mode_count), jnp.bfloat16) for _ in range(components)],
    )


def absorb(me, coeffs, group, shapes, state):
    offsets = [one[1:] for one in group]
    vmem = pl.BlockSpec(memory_space=pltpu.VMEM)
    operands = (me, coeffs, *(one[0] for one in group), *state)
    size = sum(operand.size * operand.dtype.itemsize for operand in (*operands, *shapes))
    return pl.pallas_call(
        functools.partial(take_in_kernel, offsets),
        out_shape=shapes,
        in_specs=[vmem] * len(operands),
        out_specs=(vmem,) * len(shapes),
        input_output_aliases={len(operands) - len(state) + i: i for i in range(len(state))},
        compiler_params=pltpu.CompilerParams(vmem_limit_bytes=size + 4 * 1024 * 1024),
        name="absorb",
    )(*operands)


def step_kernel(offsets, across, me_ref, coeff_ref, force_ref, visc_ref, *refs):
    chunk_refs = refs[: len(offsets)]
    out_ref, flow_ref, weight_ref, *mode_refs = refs[-3 - COMPONENTS :]
    own, mode_count = out_ref.shape
    components, devices, _, lanes = flow_ref.shape
    layers = lanes // across
    coeffs = coeff_ref[...]
    forcing = force_ref[...]
    take_in(coeffs, placing(me_ref[0, 0], offsets), chunk_refs, flow_ref, weight_ref, mode_refs)
    visc = visc_ref[...] / SLOPE_SCALE
    lane = lax.broadcasted_iota(jnp.int32, (own, lanes), 1)
    y = lane % across

    def rolled(f, by):
        return pltpu.roll(f, by % lanes, 1) if by % lanes else f

    def slope(m2, m1, p1, p2):
        return 8.0 * (p1 - m1) - (p2 - m2)

    def slope_along(field):
        def ahead(shift):
            whole, part = divmod(shift, layers)
            moved = [field[(p + whole) % devices] for p in range(devices + 1)]
            if part:
                moved = [rolled(f, -part * across) for f in moved[:devices]]
                inside = lane < (layers - part) * across
                moved = [jnp.where(inside, moved[p], moved[(p + 1) % devices]) for p in range(devices)]
            return moved[:devices]

        shifted = [ahead(s) for s in (-2, -1, 1, 2)]
        return [slope(*(s[p] for s in shifted)) for p in range(devices)]

    def slope_across(field):
        def ahead(f, shift):
            if shift > 0:
                wrapped = jnp.where(y < shift, rolled(f, across), f)
            else:
                wrapped = jnp.where(y >= across + shift, rolled(f, -across), f)
            return rolled(wrapped, -shift)

        return [slope(*(ahead(f, s) for s in (-2, -1, 1, 2))) for f in field]

    weight = [weight_ref[p : p + 1, :] for p in range(devices)]

    for repeat in range(STEPS):
        flow = []
        for a in range(components):
            if repeat == 0:
                flow.append([flow_ref[a, p] for p in range(devices)])
                continue
            high, low = halves(coeffs)
            left = jnp.concatenate(
                [jnp.concatenate([high, high], axis=1), jnp.concatenate([low, low], axis=1)], axis=0
            )
            both = lax.dot_general(
                left, mode_refs[a][...], (((1,), (1,)), ((), ())), preferred_element_type=jnp.float32
            )
            both = both[:own] + both[own:]
            flow.append([both[:, p * lanes : (p + 1) * lanes] for p in range(devices)])
        change = jnp.zeros((own, mode_count), jnp.float32)
        for a in range(components):
            x_slope = slope_along(flow[a])
            y_slope = slope_across(flow[a])
            x_flux = [weight[p] * x_slope[p] for p in range(devices)]
            y_flux = [weight[p] * y_slope[p] for p in range(devices)]
            x_spread = slope_along(x_flux)
            y_spread = slope_across(y_flux)
            source = jnp.concatenate(
                [
                    flow[0][p] * x_flux[p] + flow[1][p] * y_flux[p] - visc * (x_spread[p] + y_spread[p])
                    for p in range(devices)
                ],
                axis=1,
            )
            high, low = halves(source)
            right = jnp.dot(
                jnp.concatenate([high, low], axis=0), mode_refs[a][...], preferred_element_type=jnp.float32
            )
            right = right[:own] + right[own:]
            change = change + right[:, :mode_count] + right[:, mode_count:]
        coeffs = coeffs + TIME_STEP * (forcing - change)
    out_ref[...] = coeffs


def shards(modes, cell_weight, seeds, coeff_table, force_table, visc_table):
    components, mode_count, layers, across = modes.shape
    own = seeds.shape[0]
    lanes = layers * across
    devices = lax.axis_size("space")
    rows = select(seeds, coeff_table, force_table, visc_table)
    groups, by_offset = gather(modes, cell_weight, rows)
    me = jnp.full((1, 128), lax.axis_index("space") if by_offset else 0, jnp.int32)
    shapes = state_of(components, devices, own, lanes, mode_count)
    state = ()
    for group in groups[:-1]:
        state = absorb(me, rows[0], group, shapes, state)
    late = groups[-1]
    vmem = pl.BlockSpec(memory_space=pltpu.VMEM)
    operands = (me, *rows, *(one[0] for one in late), *state)
    size = sum(operand.size * operand.dtype.itemsize for operand in (*operands, *shapes))
    out = jax.ShapeDtypeStruct((own, mode_count), jnp.float32)
    out, *_ = pl.pallas_call(
        functools.partial(step_kernel, [one[1:] for one in late], across),
        out_shape=(out, *shapes),
        in_specs=[vmem] * len(operands),
        out_specs=(vmem,) * (1 + len(shapes)),
        input_output_aliases={len(operands) - len(state) + i: 1 + i for i in range(len(state))},
        compiler_params=pltpu.CompilerParams(vmem_limit_bytes=size + 4 * 1024 * 1024),
        name="steps",
    )(*operands)
    return out


def solution(mesh):
    placed = (
        P("groups", None, "space", None),
        P("space", "groups"),
        P(("groups", "space")),
        P(),
        P(),
        P(),
    )
    return jax.shard_map(
        shards, mesh=mesh, in_specs=placed, out_specs=P(("groups", "space"), None), check_vma=False
    )
```

```python
import functools

import jax
import jax.numpy as jnp
from jax import lax
from jax.experimental import pallas as pl
from jax.experimental.pallas import tpu as pltpu
from jax.sharding import PartitionSpec as P

STEPS = 2


TIME_STEP = 0.5
SPARE_ROWS = 8
SLOPE_SCALE = 12.0
COMPONENTS = 2


def lay_kernel(weight_ref, row_ref):
    layers, across = weight_ref.shape
    for layer in range(layers):
        row_ref[:, layer * across : (layer + 1) * across] = jnp.broadcast_to(
            weight_ref[layer : layer + 1, :], (SPARE_ROWS, across)
        )


def lay(cell_weight):
    layers, across = cell_weight.shape
    return pl.pallas_call(
        lay_kernel,
        out_shape=jax.ShapeDtypeStruct((SPARE_ROWS, layers * across), jnp.float32),
        in_specs=[pl.BlockSpec(memory_space=pltpu.VMEM)],
        out_specs=pl.BlockSpec(memory_space=pltpu.VMEM),
        compiler_params=pltpu.CompilerParams(vmem_limit_bytes=1024 * 1024),
        name="lay",
    )(cell_weight)


def pack_kernel(modes_ref, row_ref, chunk_ref):
    rows = modes_ref.shape[0]
    chunk_ref[0:rows, :] = modes_ref[...]
    chunk_ref[rows : rows + SPARE_ROWS, :] = row_ref[...]


def pack(modes, weight_rows):
    rows, mode_count = modes.shape
    return pl.pallas_call(
        pack_kernel,
        out_shape=jax.ShapeDtypeStruct((rows + SPARE_ROWS, mode_count), jnp.float32),
        in_specs=[pl.BlockSpec(memory_space=pltpu.VMEM)] * 2,
        out_specs=pl.BlockSpec(memory_space=pltpu.VMEM),
        compiler_params=pltpu.CompilerParams(vmem_limit_bytes=2 * 1024 * 1024),
        name="pack",
    )(modes, weight_rows)


def center_kernel(components, chunk_ref, center_ref):
    cells = (chunk_ref.shape[0] - SPARE_ROWS) // components
    center_ref[...] = jnp.zeros_like(center_ref)
    for a in range(components):
        rows = chunk_ref[a * cells : (a + 1) * cells, :]
        center_ref[a : a + 1, :] = jnp.sum(rows, axis=0, keepdims=True) * (1.0 / cells)


def center(chunk, components):
    vmem = pl.BlockSpec(memory_space=pltpu.VMEM)
    return pl.pallas_call(
        functools.partial(center_kernel, components),
        out_shape=jax.ShapeDtypeStruct((SPARE_ROWS, chunk.shape[1]), jnp.float32),
        in_specs=[vmem],
        out_specs=vmem,
        compiler_params=pltpu.CompilerParams(vmem_limit_bytes=1024 * 1024),
        name="center",
    )(chunk)


def exchange(held, even_mask, odd_mask):
    array, even, odd = held
    devices = lax.axis_size("space")
    pairs = [(i, i ^ (odd_mask if i & 1 else even_mask)) for i in range(devices)]
    array = lax.ppermute(array, "space", pairs)
    if even_mask & 1:
        even, odd = odd, even
    return array, even ^ even_mask, odd ^ odd_mask


def gather(modes, cell_weight, first_needed):
    components, mode_count, layers, across = modes.shape
    rows = modes.transpose(0, 2, 3, 1).reshape(components * layers * across, mode_count)
    devices = lax.axis_size("space")
    if devices < 16 or devices & (devices - 1):
        everyone = lax.all_gather(pack(rows, lay(cell_weight)), "space")
        return [[(everyone[j], j, j) for j in range(devices)]], False
    near = devices // 4
    side = near // 2
    far = devices // 2 + near
    far_rows, even, odd = exchange((rows, 0, 0), far, far)
    far_weight = exchange((cell_weight, 0, 0), far, far)[0]
    own = (pack(rows, lay(cell_weight)), 0, 0)
    far_rows, *_ = lax.optimization_barrier((far_rows, *first_needed))
    opposite = (pack(far_rows, lay(far_weight)), even, odd)
    held = []
    for start in (own, opposite):
        first = exchange(start, near, side)
        second = exchange(start, side, near)
        held += [start, first, second, exchange(first, side, near)]
    order = [0,0,0,1,0,0,0,2]
    mask = side // 2
    while mask:
        held += [exchange(one, mask, mask) for one in held]
        order += order
        mask //= 2
    groups = [[one for one, at in zip(held, order) if at == wanted] for wanted in range(3)]
    return groups, True


def halves(array):
    high = array.astype(jnp.bfloat16)
    low = (array - high.astype(jnp.float32)).astype(jnp.bfloat16)
    return high, low


def select_kernel(seeds_ref, visc_table_ref, coeff_table_ref, force_table_ref, coeff_ref, force_ref, visc_ref):
    own, mode_count = coeff_ref.shape
    row_id = lax.broadcasted_iota(jnp.int32, (own, mode_count), 0)
    visc = jnp.zeros((own, mode_count), jnp.float32)
    for n in range(own):
        seed = seeds_ref[n]
        coeff_ref[n : n + 1, :] = coeff_table_ref[pl.ds(seed, 1), :]
        force_ref[n : n + 1, :] = force_table_ref[pl.ds(seed, 1), :]
        visc = jnp.where(row_id == n, visc_table_ref[seed], visc)
    visc_ref[...] = visc


def select(seeds, coeff_table, force_table, visc_table):
    smem = pl.BlockSpec(memory_space=pltpu.SMEM)
    vmem = pl.BlockSpec(memory_space=pltpu.VMEM)
    rows = jax.ShapeDtypeStruct((seeds.shape[0], coeff_table.shape[1]), jnp.float32)
    return pl.pallas_call(
        select_kernel,
        out_shape=(rows, rows, rows),
        in_specs=[smem, smem, vmem, vmem],
        out_specs=(vmem, vmem, vmem),
        compiler_params=pltpu.CompilerParams(vmem_limit_bytes=2 * 1024 * 1024),
        name="select",
    )(seeds, visc_table, coeff_table, force_table)


def placing(me, offsets):
    odd = me % 2 == 1
    return [jnp.bitwise_xor(me, jnp.where(odd, odd_offset, even_offset)) for even_offset, odd_offset in offsets]


def take_in(coeffs, center_ref, places, chunk_refs, flow_ref, weight_ref, mode_refs):
    own, mode_count = coeffs.shape
    components, devices, _, lanes = flow_ref.shape
    total_cells = devices * lanes
    high, low = halves(coeffs)
    left = jnp.concatenate([jnp.concatenate([high, high], axis=1), jnp.concatenate([low, low], axis=1)], axis=0)
    for place, chunk_ref in zip(places, chunk_refs):
        rows = pl.ds(pl.multiple_of(place * lanes, lanes), lanes)
        for a in range(components):
            beyond = chunk_ref[a * lanes : (a + 1) * lanes, :] - center_ref[a : a + 1, :]
            split = jnp.concatenate(halves(beyond), axis=1)
            mode_refs[a][rows, :] = split
            both = lax.dot_general(left, split, (((1,), (1,)), ((), ())), preferred_element_type=jnp.float32)
            flow_ref[a, place] = both[:own] + both[own:]
        last = components * lanes
        weight_ref[pl.ds(place, 1), :] = chunk_ref[last : last + 1, :] / (SLOPE_SCALE * total_cells)


def take_in_kernel(offsets, me_ref, coeff_ref, center_ref, *refs):
    chunk_refs = refs[: len(offsets)]
    kept = refs[-2 - COMPONENTS :]
    take_in(coeff_ref[...], center_ref, placing(me_ref[0, 0], offsets), chunk_refs, kept[0], kept[1], kept[2:])


def state_of(components, devices, own, lanes, mode_count):
    return (
        jax.ShapeDtypeStruct((components, devices, own, lanes), jnp.float32),
        jax.ShapeDtypeStruct((devices, lanes), jnp.float32),
        *[jax.ShapeDtypeStruct((devices * lanes, 2 * mode_count), jnp.bfloat16) for _ in range(components)],
    )


def absorb(me, coeffs, middle, group, shapes, state):
    offsets = [one[1:] for one in group]
    vmem = pl.BlockSpec(memory_space=pltpu.VMEM)
    operands = (me, coeffs, middle, *(one[0] for one in group), *state)
    size = sum(operand.size * operand.dtype.itemsize for operand in (*operands, *shapes))
    return pl.pallas_call(
        functools.partial(take_in_kernel, offsets),
        out_shape=shapes,
        in_specs=[vmem] * len(operands),
        out_specs=(vmem,) * len(shapes),
        input_output_aliases={len(operands) - len(state) + i: i for i in range(len(state))},
        compiler_params=pltpu.CompilerParams(vmem_limit_bytes=size + 4 * 1024 * 1024),
        name="absorb",
    )(*operands)


def step_kernel(offsets, across, me_ref, coeff_ref, force_ref, visc_ref, center_ref, *refs):
    chunk_refs = refs[: len(offsets)]
    out_ref, flow_ref, weight_ref, *mode_refs = refs[-3 - COMPONENTS :]
    own, mode_count = out_ref.shape
    components, devices, _, lanes = flow_ref.shape
    layers = lanes // across
    coeffs = coeff_ref[...]
    forcing = force_ref[...]
    take_in(coeffs, center_ref, placing(me_ref[0, 0], offsets), chunk_refs, flow_ref, weight_ref, mode_refs)
    visc = visc_ref[...] / SLOPE_SCALE
    lane = lax.broadcasted_iota(jnp.int32, (own, lanes), 1)
    y = lane % across

    def rolled(f, by):
        return pltpu.roll(f, by % lanes, 1) if by % lanes else f

    def slope(m2, m1, p1, p2):
        return 8.0 * (p1 - m1) - (p2 - m2)

    def slope_along(field):
        def ahead(shift):
            whole, part = divmod(shift, layers)
            moved = [field[(p + whole) % devices] for p in range(devices + 1)]
            if part:
                moved = [rolled(f, -part * across) for f in moved[:devices]]
                inside = lane < (layers - part) * across
                moved = [jnp.where(inside, moved[p], moved[(p + 1) % devices]) for p in range(devices)]
            return moved[:devices]

        shifted = [ahead(s) for s in (-2, -1, 1, 2)]
        return [slope(*(s[p] for s in shifted)) for p in range(devices)]

    def slope_across(field):
        def ahead(f, shift):
            if shift > 0:
                wrapped = jnp.where(y < shift, rolled(f, across), f)
            else:
                wrapped = jnp.where(y >= across + shift, rolled(f, -across), f)
            return rolled(wrapped, -shift)

        return [slope(*(ahead(f, s) for s in (-2, -1, 1, 2))) for f in field]

    weight = [weight_ref[p : p + 1, :] for p in range(devices)]

    for repeat in range(STEPS):
        flow = []
        for a in range(components):
            if repeat == 0:
                flow.append([flow_ref[a, p] for p in range(devices)])
                continue
            high, low = halves(coeffs)
            left = jnp.concatenate(
                [jnp.concatenate([high, high], axis=1), jnp.concatenate([low, low], axis=1)], axis=0
            )
            both = lax.dot_general(
                left, mode_refs[a][...], (((1,), (1,)), ((), ())), preferred_element_type=jnp.float32
            )
            both = both[:own] + both[own:]
            flow.append([both[:, p * lanes : (p + 1) * lanes] for p in range(devices)])
        centers = [center_ref[a : a + 1, :] for a in range(components)]
        base = [jnp.sum(coeffs * centers[a], axis=1, keepdims=True) for a in range(components)]
        whole = [[f + base[a] for f in flow[a]] for a in range(components)]
        change = jnp.zeros((own, mode_count), jnp.float32)
        for a in range(components):
            x_slope = slope_along(flow[a])
            y_slope = slope_across(flow[a])
            x_flux = [weight[p] * x_slope[p] for p in range(devices)]
            y_flux = [weight[p] * y_slope[p] for p in range(devices)]
            x_spread = slope_along(x_flux)
            y_spread = slope_across(y_flux)
            source = [
                whole[0][p] * x_flux[p] + whole[1][p] * y_flux[p] - visc * (x_spread[p] + y_spread[p])
                for p in range(devices)
            ]
            change = change + jnp.sum(sum(source), axis=1, keepdims=True) * centers[a]
            high, low = halves(jnp.concatenate(source, axis=1))
            right = jnp.dot(
                jnp.concatenate([high, low], axis=0), mode_refs[a][...], preferred_element_type=jnp.float32
            )
            right = right[:own] + right[own:]
            change = change + right[:, :mode_count] + right[:, mode_count:]
        coeffs = coeffs + TIME_STEP * (forcing - change)
    out_ref[...] = coeffs


def shards(modes, cell_weight, seeds, coeff_table, force_table, visc_table):
    components, mode_count, layers, across = modes.shape
    own = seeds.shape[0]
    lanes = layers * across
    devices = lax.axis_size("space")
    rows = select(seeds, coeff_table, force_table, visc_table)
    groups, by_offset = gather(modes, cell_weight, rows)
    me = jnp.full((1, 128), lax.axis_index("space") if by_offset else 0, jnp.int32)
    middle = center(groups[0][0][0], components)
    shapes = state_of(components, devices, own, lanes, mode_count)
    state = ()
    for group in groups[:-1]:
        state = absorb(me, rows[0], middle, group, shapes, state)
    late = groups[-1]
    vmem = pl.BlockSpec(memory_space=pltpu.VMEM)
    operands = (me, *rows, middle, *(one[0] for one in late), *state)
    size = sum(operand.size * operand.dtype.itemsize for operand in (*operands, *shapes))
    out = jax.ShapeDtypeStruct((own, mode_count), jnp.float32)
    out, *_ = pl.pallas_call(
        functools.partial(step_kernel, [one[1:] for one in late], across),
        out_shape=(out, *shapes),
        in_specs=[vmem] * len(operands),
        out_specs=(vmem,) * (1 + len(shapes)),
        input_output_aliases={len(operands) - len(state) + i: 1 + i for i in range(len(state))},
        compiler_params=pltpu.CompilerParams(vmem_limit_bytes=size + 4 * 1024 * 1024),
        name="steps",
    )(*operands)
    return out


def solution(mesh):
    placed = (
        P("groups", None, "space", None),
        P("space", "groups"),
        P(("groups", "space")),
        P(),
        P(),
        P(),
    )
    return jax.shard_map(
        shards, mesh=mesh, in_specs=placed, out_specs=P(("groups", "space"), None), check_vma=False
    )
```

```python
import functools

import jax
import jax.numpy as jnp
from jax import lax
from jax.experimental import pallas as pl
from jax.experimental.pallas import tpu as pltpu
from jax.sharding import PartitionSpec as P

STEPS = 2


TIME_STEP = 0.5
SPARE_ROWS = 8
SLOPE_SCALE = 12.0
COMPONENTS = 2
COPIES_LIMIT = 8 * 1024 * 1024


def lay_kernel(weight_ref, row_ref):
    layers, across = weight_ref.shape
    for layer in range(layers):
        row_ref[:, layer * across : (layer + 1) * across] = jnp.broadcast_to(
            weight_ref[layer : layer + 1, :], (SPARE_ROWS, across)
        )


def lay(cell_weight):
    layers, across = cell_weight.shape
    return pl.pallas_call(
        lay_kernel,
        out_shape=jax.ShapeDtypeStruct((SPARE_ROWS, layers * across), jnp.float32),
        in_specs=[pl.BlockSpec(memory_space=pltpu.VMEM)],
        out_specs=pl.BlockSpec(memory_space=pltpu.VMEM),
        compiler_params=pltpu.CompilerParams(vmem_limit_bytes=1024 * 1024),
        name="lay",
    )(cell_weight)


def pack_kernel(modes_ref, row_ref, chunk_ref):
    rows = modes_ref.shape[0]
    chunk_ref[0:rows, :] = modes_ref[...]
    chunk_ref[rows : rows + SPARE_ROWS, :] = row_ref[...]


def pack(modes, weight_rows):
    rows, mode_count = modes.shape
    return pl.pallas_call(
        pack_kernel,
        out_shape=jax.ShapeDtypeStruct((rows + SPARE_ROWS, mode_count), jnp.float32),
        in_specs=[pl.BlockSpec(memory_space=pltpu.VMEM)] * 2,
        out_specs=pl.BlockSpec(memory_space=pltpu.VMEM),
        compiler_params=pltpu.CompilerParams(vmem_limit_bytes=2 * 1024 * 1024),
        name="pack",
    )(modes, weight_rows)


def center_kernel(components, chunk_ref, center_ref):
    cells = (chunk_ref.shape[0] - SPARE_ROWS) // components
    center_ref[...] = jnp.zeros_like(center_ref)
    for a in range(components):
        rows = chunk_ref[a * cells : (a + 1) * cells, :]
        center_ref[a : a + 1, :] = jnp.sum(rows, axis=0, keepdims=True) * (1.0 / cells)


def center(chunk, components):
    vmem = pl.BlockSpec(memory_space=pltpu.VMEM)
    return pl.pallas_call(
        functools.partial(center_kernel, components),
        out_shape=jax.ShapeDtypeStruct((SPARE_ROWS, chunk.shape[1]), jnp.float32),
        in_specs=[vmem],
        out_specs=vmem,
        compiler_params=pltpu.CompilerParams(vmem_limit_bytes=1024 * 1024),
        name="center",
    )(chunk)


def exchange(held, even_mask, odd_mask):
    array, even, odd = held
    devices = lax.axis_size("space")
    pairs = [(i, i ^ (odd_mask if i & 1 else even_mask)) for i in range(devices)]
    array = lax.ppermute(array, "space", pairs)
    if even_mask & 1:
        even, odd = odd, even
    return array, even ^ even_mask, odd ^ odd_mask


def gather(modes, cell_weight, first_needed):
    components, mode_count, layers, across = modes.shape
    rows = modes.transpose(0, 2, 3, 1).reshape(components * layers * across, mode_count)
    devices = lax.axis_size("space")
    if devices < 16 or devices & (devices - 1):
        everyone = lax.all_gather(pack(rows, lay(cell_weight)), "space")
        return [[(everyone[j], j, j) for j in range(devices)]], False
    near = devices // 4
    side = near // 2
    far = devices // 2 + near
    far_rows, even, odd = exchange((rows, 0, 0), far, far)
    far_weight = exchange((cell_weight, 0, 0), far, far)[0]
    own = (pack(rows, lay(cell_weight)), 0, 0)
    far_rows, *_ = lax.optimization_barrier((far_rows, *first_needed))
    opposite = (pack(far_rows, lay(far_weight)), even, odd)
    held = []
    for start in (own, opposite):
        first = exchange(start, near, side)
        second = exchange(start, side, near)
        held += [start, first, second, exchange(first, side, near)]
    order = [0,0,0,1,0,0,0,2]
    mask = side // 2
    while mask:
        held += [exchange(one, mask, mask) for one in held]
        order += order
        mask //= 2
    groups = [[one for one, at in zip(held, order) if at == wanted] for wanted in range(3)]
    return groups, True


def halves(array):
    high = array.astype(jnp.bfloat16)
    low = (array - high.astype(jnp.float32)).astype(jnp.bfloat16)
    return high, low


def select_kernel(seeds_ref, visc_table_ref, coeff_table_ref, force_table_ref, coeff_ref, force_ref, visc_ref):
    own, mode_count = coeff_ref.shape
    row_id = lax.broadcasted_iota(jnp.int32, (own, mode_count), 0)
    visc = jnp.zeros((own, mode_count), jnp.float32)
    for n in range(own):
        seed = seeds_ref[n]
        coeff_ref[n : n + 1, :] = coeff_table_ref[pl.ds(seed, 1), :]
        force_ref[n : n + 1, :] = force_table_ref[pl.ds(seed, 1), :]
        visc = jnp.where(row_id == n, visc_table_ref[seed], visc)
    visc_ref[...] = visc


def select(seeds, coeff_table, force_table, visc_table):
    smem = pl.BlockSpec(memory_space=pltpu.SMEM)
    vmem = pl.BlockSpec(memory_space=pltpu.VMEM)
    rows = jax.ShapeDtypeStruct((seeds.shape[0], coeff_table.shape[1]), jnp.float32)
    return pl.pallas_call(
        select_kernel,
        out_shape=(rows, rows, rows),
        in_specs=[smem, smem, vmem, vmem],
        out_specs=(vmem, vmem, vmem),
        compiler_params=pltpu.CompilerParams(vmem_limit_bytes=2 * 1024 * 1024),
        name="select",
    )(seeds, visc_table, coeff_table, force_table)


def placing(me, offsets):
    odd = me % 2 == 1
    return [jnp.bitwise_xor(me, jnp.where(odd, odd_offset, even_offset)) for even_offset, odd_offset in offsets]


def take_in(coeffs, center_ref, places, chunk_refs, flow_ref, weight_ref, mode_refs):
    own, mode_count = coeffs.shape
    components, devices, _, lanes = flow_ref.shape
    total_cells = devices * lanes
    high, low = halves(coeffs)
    left = jnp.concatenate([jnp.concatenate([high, high], axis=1), jnp.concatenate([low, low], axis=1)], axis=0)
    for place, chunk_ref in zip(places, chunk_refs):
        rows = pl.ds(pl.multiple_of(place * lanes, lanes), lanes)
        for a in range(components):
            beyond = chunk_ref[a * lanes : (a + 1) * lanes, :] - center_ref[a : a + 1, :]
            split = jnp.concatenate(halves(beyond), axis=1)
            mode_refs[a][rows, :] = split
            if len(mode_refs) > components:
                mode_refs[components + a][:, rows] = jnp.concatenate(halves(beyond.T), axis=0)
            both = lax.dot_general(left, split, (((1,), (1,)), ((), ())), preferred_element_type=jnp.float32)
            flow_ref[a, place] = both[:own] + both[own:]
        last = components * lanes
        weight_ref[pl.ds(place, 1), :] = chunk_ref[last : last + 1, :] / (SLOPE_SCALE * total_cells)


def take_in_kernel(offsets, copies, me_ref, coeff_ref, center_ref, *refs):
    chunk_refs = refs[: len(offsets)]
    kept = refs[-2 - copies * COMPONENTS :]
    take_in(coeff_ref[...], center_ref, placing(me_ref[0, 0], offsets), chunk_refs, kept[0], kept[1], kept[2:])


def state_of(copies, components, devices, own, lanes, mode_count):
    return (
        jax.ShapeDtypeStruct((components, devices, own, lanes), jnp.float32),
        jax.ShapeDtypeStruct((devices, lanes), jnp.float32),
        *[
            jax.ShapeDtypeStruct(shape, jnp.bfloat16)
            for shape in ((devices * lanes, 2 * mode_count), (2 * mode_count, devices * lanes))[:copies]
            for _ in range(components)
        ],
    )


def absorb(copies, me, coeffs, middle, group, shapes, state):
    offsets = [one[1:] for one in group]
    vmem = pl.BlockSpec(memory_space=pltpu.VMEM)
    operands = (me, coeffs, middle, *(one[0] for one in group), *state)
    size = sum(operand.size * operand.dtype.itemsize for operand in (*operands, *shapes))
    return pl.pallas_call(
        functools.partial(take_in_kernel, offsets, copies),
        out_shape=shapes,
        in_specs=[vmem] * len(operands),
        out_specs=(vmem,) * len(shapes),
        input_output_aliases={len(operands) - len(state) + i: i for i in range(len(state))},
        compiler_params=pltpu.CompilerParams(vmem_limit_bytes=size + 4 * 1024 * 1024),
        name="absorb",
    )(*operands)


def step_kernel(offsets, copies, across, me_ref, coeff_ref, force_ref, visc_ref, center_ref, *refs):
    chunk_refs = refs[: len(offsets)]
    out_ref, flow_ref, weight_ref, *mode_refs = refs[-3 - copies * COMPONENTS :]
    own, mode_count = out_ref.shape
    components, devices, _, lanes = flow_ref.shape
    layers = lanes // across
    coeffs = coeff_ref[...]
    forcing = force_ref[...]
    take_in(coeffs, center_ref, placing(me_ref[0, 0], offsets), chunk_refs, flow_ref, weight_ref, mode_refs)
    visc = visc_ref[...] / SLOPE_SCALE
    lane = lax.broadcasted_iota(jnp.int32, (own, lanes), 1)
    y = lane % across

    def rolled(f, by):
        return pltpu.roll(f, by % lanes, 1) if by % lanes else f

    def slope(m2, m1, p1, p2):
        return 8.0 * (p1 - m1) - (p2 - m2)

    def slope_along(field):
        def ahead(shift):
            whole, part = divmod(shift, layers)
            moved = [field[(p + whole) % devices] for p in range(devices + 1)]
            if part:
                moved = [rolled(f, -part * across) for f in moved[:devices]]
                inside = lane < (layers - part) * across
                moved = [jnp.where(inside, moved[p], moved[(p + 1) % devices]) for p in range(devices)]
            return moved[:devices]

        shifted = [ahead(s) for s in (-2, -1, 1, 2)]
        return [slope(*(s[p] for s in shifted)) for p in range(devices)]

    def slope_across(field):
        def ahead(f, shift):
            if shift > 0:
                wrapped = jnp.where(y < shift, rolled(f, across), f)
            else:
                wrapped = jnp.where(y >= across + shift, rolled(f, -across), f)
            return rolled(wrapped, -shift)

        return [slope(*(ahead(f, s) for s in (-2, -1, 1, 2))) for f in field]

    weight = [weight_ref[p : p + 1, :] for p in range(devices)]

    centers = [center_ref[a : a + 1, :] for a in range(components)]
    for repeat in range(STEPS):
        high, low = halves(coeffs)
        left = jnp.concatenate(
            [jnp.concatenate([high, high], axis=1), jnp.concatenate([low, low], axis=1)], axis=0
        )
        whole = []
        fluxes = []
        for a in range(components):
            if repeat == 0:
                flow = [flow_ref[a, p] for p in range(devices)]
            else:
                if copies > 1:
                    both = jnp.dot(left, mode_refs[components + a][...], preferred_element_type=jnp.float32)
                else:
                    both = lax.dot_general(
                        left, mode_refs[a][...], (((1,), (1,)), ((), ())), preferred_element_type=jnp.float32
                    )
                both = both[:own] + both[own:]
                flow = [both[:, p * lanes : (p + 1) * lanes] for p in range(devices)]
            base = jnp.sum(coeffs * centers[a], axis=1, keepdims=True)
            whole.append([f + base for f in flow])
            x_slope = slope_along(flow)
            y_slope = slope_across(flow)
            x_flux = [weight[p] * x_slope[p] for p in range(devices)]
            y_flux = [weight[p] * y_slope[p] for p in range(devices)]
            x_spread = slope_along(x_flux)
            y_spread = slope_across(y_flux)
            viscous = [visc * (x_spread[p] + y_spread[p]) for p in range(devices)]
            fluxes.append((x_flux, y_flux, viscous))
        change = jnp.zeros((own, mode_count), jnp.float32)
        for a, (x_flux, y_flux, viscous) in enumerate(fluxes):
            source = [whole[0][p] * x_flux[p] + whole[1][p] * y_flux[p] - viscous[p] for p in range(devices)]
            change = change + jnp.sum(sum(source), axis=1, keepdims=True) * centers[a]
            high, low = halves(jnp.concatenate(source, axis=1))
            right = jnp.dot(
                jnp.concatenate([high, low], axis=0), mode_refs[a][...], preferred_element_type=jnp.float32
            )
            right = right[:own] + right[own:]
            change = change + right[:, :mode_count] + right[:, mode_count:]
        coeffs = coeffs + TIME_STEP * (forcing - change)
    out_ref[...] = coeffs


def shards(modes, cell_weight, seeds, coeff_table, force_table, visc_table):
    components, mode_count, layers, across = modes.shape
    own = seeds.shape[0]
    lanes = layers * across
    devices = lax.axis_size("space")
    rows = select(seeds, coeff_table, force_table, visc_table)
    groups, by_offset = gather(modes, cell_weight, rows)
    me = jnp.full((1, 128), lax.axis_index("space") if by_offset else 0, jnp.int32)
    middle = center(groups[0][0][0], components)
    copies = 2 if 8 * components * devices * lanes * mode_count <= COPIES_LIMIT else 1
    shapes = state_of(copies, components, devices, own, lanes, mode_count)
    state = ()
    for group in groups[:-1]:
        state = absorb(copies, me, rows[0], middle, group, shapes, state)
    late = groups[-1]
    vmem = pl.BlockSpec(memory_space=pltpu.VMEM)
    operands = (me, *rows, middle, *(one[0] for one in late), *state)
    size = sum(operand.size * operand.dtype.itemsize for operand in (*operands, *shapes))
    out = jax.ShapeDtypeStruct((own, mode_count), jnp.float32)
    out, *_ = pl.pallas_call(
        functools.partial(step_kernel, [one[1:] for one in late], copies, across),
        out_shape=(out, *shapes),
        in_specs=[vmem] * len(operands),
        out_specs=(vmem,) * (1 + len(shapes)),
        input_output_aliases={len(operands) - len(state) + i: 1 + i for i in range(len(state))},
        compiler_params=pltpu.CompilerParams(vmem_limit_bytes=size + 4 * 1024 * 1024),
        name="steps",
    )(*operands)
    return out


def solution(mesh):
    placed = (
        P("groups", None, "space", None),
        P("space", "groups"),
        P(("groups", "space")),
        P(),
        P(),
        P(),
    )
    return jax.shard_map(
        shards, mesh=mesh, in_specs=placed, out_specs=P(("groups", "space"), None), check_vma=False
    )
```

```python
import functools

import jax
import jax.numpy as jnp
from jax import lax
from jax.experimental import pallas as pl
from jax.experimental.pallas import tpu as pltpu
from jax.sharding import PartitionSpec as P

STEPS = 2


TIME_STEP = 0.5
SPARE_ROWS = 8
SLOPE_SCALE = 12.0
COMPONENTS = 2
COPIES_LIMIT = 8 * 1024 * 1024


def lay_kernel(weight_ref, row_ref):
    layers, across = weight_ref.shape
    for layer in range(layers):
        row_ref[:, layer * across : (layer + 1) * across] = jnp.broadcast_to(
            weight_ref[layer : layer + 1, :], (SPARE_ROWS, across)
        )


def lay(cell_weight):
    layers, across = cell_weight.shape
    return pl.pallas_call(
        lay_kernel,
        out_shape=jax.ShapeDtypeStruct((SPARE_ROWS, layers * across), jnp.float32),
        in_specs=[pl.BlockSpec(memory_space=pltpu.VMEM)],
        out_specs=pl.BlockSpec(memory_space=pltpu.VMEM),
        compiler_params=pltpu.CompilerParams(vmem_limit_bytes=1024 * 1024),
        name="lay",
    )(cell_weight)


def pack_kernel(modes_ref, weight_ref, chunk_ref):
    rows = modes_ref.shape[0]
    chunk_ref[0:rows, :] = modes_ref[...]
    if weight_ref.shape == (SPARE_ROWS, modes_ref.shape[1]):
        chunk_ref[rows : rows + SPARE_ROWS, :] = weight_ref[...]
    else:
        lay_kernel(weight_ref, chunk_ref.at[rows : rows + SPARE_ROWS, :])


def pack(modes, weight_rows):
    rows, mode_count = modes.shape
    return pl.pallas_call(
        pack_kernel,
        out_shape=jax.ShapeDtypeStruct((rows + SPARE_ROWS, mode_count), jnp.float32),
        in_specs=[pl.BlockSpec(memory_space=pltpu.VMEM)] * 2,
        out_specs=pl.BlockSpec(memory_space=pltpu.VMEM),
        compiler_params=pltpu.CompilerParams(vmem_limit_bytes=2 * 1024 * 1024),
        name="pack",
    )(modes, weight_rows)


def center_kernel(components, chunk_ref, center_ref):
    cells = (chunk_ref.shape[0] - SPARE_ROWS) // components
    center_ref[...] = jnp.zeros_like(center_ref)
    for a in range(components):
        rows = chunk_ref[a * cells : (a + 1) * cells, :]
        center_ref[a : a + 1, :] = jnp.sum(rows, axis=0, keepdims=True) * (1.0 / cells)


def center(chunk, components):
    vmem = pl.BlockSpec(memory_space=pltpu.VMEM)
    return pl.pallas_call(
        functools.partial(center_kernel, components),
        out_shape=jax.ShapeDtypeStruct((SPARE_ROWS, chunk.shape[1]), jnp.float32),
        in_specs=[vmem],
        out_specs=vmem,
        compiler_params=pltpu.CompilerParams(vmem_limit_bytes=1024 * 1024),
        name="center",
    )(chunk)


def exchange(held, even_mask, odd_mask):
    array, even, odd = held
    devices = lax.axis_size("space")
    pairs = [(i, i ^ (odd_mask if i & 1 else even_mask)) for i in range(devices)]
    array = lax.ppermute(array, "space", pairs)
    if even_mask & 1:
        even, odd = odd, even
    return array, even ^ even_mask, odd ^ odd_mask


def gather(modes, cell_weight, first_needed):
    components, mode_count, layers, across = modes.shape
    rows = modes.transpose(0, 2, 3, 1).reshape(components * layers * across, mode_count)
    devices = lax.axis_size("space")
    if devices < 16 or devices & (devices - 1):
        everyone = lax.all_gather(pack(rows, lay(cell_weight)), "space")
        return [[(everyone[j], j, j) for j in range(devices)]], False
    near = devices // 4
    side = near // 2
    far = devices // 2 + near
    far_rows, even, odd = exchange((rows, 0, 0), far, far)
    far_weight = exchange((cell_weight, 0, 0), far, far)[0]
    own = (pack(rows, lay(cell_weight)), 0, 0)
    far_rows, *_ = lax.optimization_barrier((far_rows, *first_needed))
    opposite = (pack(far_rows, far_weight), even, odd)
    held = []
    for start in (own, opposite):
        first = exchange(start, near, side)
        second = exchange(start, side, near)
        held += [start, first, second, exchange(first, side, near)]
    order = [0,0,0,1,0,0,0,2]
    mask = side // 2
    while mask:
        held += [exchange(one, mask, mask) for one in held]
        order += order
        mask //= 2
    groups = [[one for one, at in zip(held, order) if at == wanted] for wanted in range(3)]
    return groups, True


def halves(array):
    high = array.astype(jnp.bfloat16)
    low = (array - high.astype(jnp.float32)).astype(jnp.bfloat16)
    return high, low


def select_kernel(seeds_ref, visc_table_ref, coeff_table_ref, force_table_ref, coeff_ref, force_ref, visc_ref):
    own, mode_count = coeff_ref.shape
    row_id = lax.broadcasted_iota(jnp.int32, (own, mode_count), 0)
    visc = jnp.zeros((own, mode_count), jnp.float32)
    for n in range(own):
        seed = seeds_ref[n]
        coeff_ref[n : n + 1, :] = coeff_table_ref[pl.ds(seed, 1), :]
        force_ref[n : n + 1, :] = force_table_ref[pl.ds(seed, 1), :]
        visc = jnp.where(row_id == n, visc_table_ref[seed], visc)
    visc_ref[...] = visc


def select(seeds, coeff_table, force_table, visc_table):
    smem = pl.BlockSpec(memory_space=pltpu.SMEM)
    vmem = pl.BlockSpec(memory_space=pltpu.VMEM)
    rows = jax.ShapeDtypeStruct((seeds.shape[0], coeff_table.shape[1]), jnp.float32)
    return pl.pallas_call(
        select_kernel,
        out_shape=(rows, rows, rows),
        in_specs=[smem, smem, vmem, vmem],
        out_specs=(vmem, vmem, vmem),
        compiler_params=pltpu.CompilerParams(vmem_limit_bytes=2 * 1024 * 1024),
        name="select",
    )(seeds, visc_table, coeff_table, force_table)


def placing(me, offsets):
    odd = me % 2 == 1
    return [jnp.bitwise_xor(me, jnp.where(odd, odd_offset, even_offset)) for even_offset, odd_offset in offsets]


def take_in(coeffs, center_ref, places, chunk_refs, flow_ref, weight_ref, mode_refs):
    own, mode_count = coeffs.shape
    components, devices, _, lanes = flow_ref.shape
    total_cells = devices * lanes
    high, low = halves(coeffs)
    left = jnp.concatenate([jnp.concatenate([high, high], axis=1), jnp.concatenate([low, low], axis=1)], axis=0)
    for place, chunk_ref in zip(places, chunk_refs):
        rows = pl.ds(pl.multiple_of(place * lanes, lanes), lanes)
        for a in range(components):
            beyond = chunk_ref[a * lanes : (a + 1) * lanes, :] - center_ref[a : a + 1, :]
            split = jnp.concatenate(halves(beyond), axis=1)
            mode_refs[a][rows, :] = split
            if len(mode_refs) > components:
                mode_refs[components + a][:, rows] = jnp.concatenate(halves(beyond.T), axis=0)
            both = lax.dot_general(left, split, (((1,), (1,)), ((), ())), preferred_element_type=jnp.float32)
            flow_ref[a, place] = both[:own] + both[own:]
        last = components * lanes
        weight_ref[pl.ds(place, 1), :] = chunk_ref[last : last + 1, :] / (SLOPE_SCALE * total_cells)


def take_in_kernel(offsets, copies, me_ref, coeff_ref, center_ref, *refs):
    chunk_refs = refs[: len(offsets)]
    kept = refs[-2 - copies * COMPONENTS :]
    take_in(coeff_ref[...], center_ref, placing(me_ref[0, 0], offsets), chunk_refs, kept[0], kept[1], kept[2:])


def state_of(copies, components, devices, own, lanes, mode_count):
    return (
        jax.ShapeDtypeStruct((components, devices, own, lanes), jnp.float32),
        jax.ShapeDtypeStruct((devices, lanes), jnp.float32),
        *[
            jax.ShapeDtypeStruct(shape, jnp.bfloat16)
            for shape in ((devices * lanes, 2 * mode_count), (2 * mode_count, devices * lanes))[:copies]
            for _ in range(components)
        ],
    )


def absorb(copies, me, coeffs, middle, group, shapes, state):
    offsets = [one[1:] for one in group]
    vmem = pl.BlockSpec(memory_space=pltpu.VMEM)
    operands = (me, coeffs, middle, *(one[0] for one in group), *state)
    size = sum(operand.size * operand.dtype.itemsize for operand in (*operands, *shapes))
    return pl.pallas_call(
        functools.partial(take_in_kernel, offsets, copies),
        out_shape=shapes,
        in_specs=[vmem] * len(operands),
        out_specs=(vmem,) * len(shapes),
        input_output_aliases={len(operands) - len(state) + i: i for i in range(len(state))},
        compiler_params=pltpu.CompilerParams(vmem_limit_bytes=size + 4 * 1024 * 1024),
        name="absorb",
    )(*operands)


def step_kernel(offsets, copies, across, me_ref, coeff_ref, force_ref, visc_ref, center_ref, *refs):
    chunk_refs = refs[: len(offsets)]
    out_ref, flow_ref, weight_ref, *mode_refs = refs[-3 - copies * COMPONENTS :]
    own, mode_count = out_ref.shape
    components, devices, _, lanes = flow_ref.shape
    layers = lanes // across
    coeffs = coeff_ref[...]
    forcing = force_ref[...]
    take_in(coeffs, center_ref, placing(me_ref[0, 0], offsets), chunk_refs, flow_ref, weight_ref, mode_refs)
    visc = visc_ref[...] / SLOPE_SCALE
    lane = lax.broadcasted_iota(jnp.int32, (own, lanes), 1)
    y = lane % across

    def rolled(f, by):
        return pltpu.roll(f, by % lanes, 1) if by % lanes else f

    def slope(m2, m1, p1, p2):
        return 8.0 * (p1 - m1) - (p2 - m2)

    def slope_along(field):
        def ahead(shift):
            whole, part = divmod(shift, layers)
            moved = [field[(p + whole) % devices] for p in range(devices + 1)]
            if part:
                moved = [rolled(f, -part * across) for f in moved[:devices]]
                inside = lane < (layers - part) * across
                moved = [jnp.where(inside, moved[p], moved[(p + 1) % devices]) for p in range(devices)]
            return moved[:devices]

        shifted = [ahead(s) for s in (-2, -1, 1, 2)]
        return [slope(*(s[p] for s in shifted)) for p in range(devices)]

    def slope_across(field):
        def ahead(f, shift):
            if shift > 0:
                wrapped = jnp.where(y < shift, rolled(f, across), f)
            else:
                wrapped = jnp.where(y >= across + shift, rolled(f, -across), f)
            return rolled(wrapped, -shift)

        return [slope(*(ahead(f, s) for s in (-2, -1, 1, 2))) for f in field]

    weight = [weight_ref[p : p + 1, :] for p in range(devices)]

    centers = [center_ref[a : a + 1, :] for a in range(components)]
    for repeat in range(STEPS):
        high, low = halves(coeffs)
        left = jnp.concatenate(
            [jnp.concatenate([high, high], axis=1), jnp.concatenate([low, low], axis=1)], axis=0
        )
        whole = []
        fluxes = []
        for a in range(components):
            if repeat == 0:
                flow = [flow_ref[a, p] for p in range(devices)]
            else:
                if copies > 1:
                    both = jnp.dot(left, mode_refs[components + a][...], preferred_element_type=jnp.float32)
                else:
                    both = lax.dot_general(
                        left, mode_refs[a][...], (((1,), (1,)), ((), ())), preferred_element_type=jnp.float32
                    )
                both = both[:own] + both[own:]
                flow = [both[:, p * lanes : (p + 1) * lanes] for p in range(devices)]
            base = jnp.sum(coeffs * centers[a], axis=1, keepdims=True)
            whole.append([f + base for f in flow])
            x_slope = slope_along(flow)
            y_slope = slope_across(flow)
            x_flux = [weight[p] * x_slope[p] for p in range(devices)]
            y_flux = [weight[p] * y_slope[p] for p in range(devices)]
            x_spread = slope_along(x_flux)
            y_spread = slope_across(y_flux)
            viscous = [visc * (x_spread[p] + y_spread[p]) for p in range(devices)]
            fluxes.append((x_flux, y_flux, viscous))
        change = jnp.zeros((own, mode_count), jnp.float32)
        for a, (x_flux, y_flux, viscous) in enumerate(fluxes):
            source = [whole[0][p] * x_flux[p] + whole[1][p] * y_flux[p] - viscous[p] for p in range(devices)]
            change = change + jnp.sum(sum(source), axis=1, keepdims=True) * centers[a]
            high, low = halves(jnp.concatenate(source, axis=1))
            right = jnp.dot(
                jnp.concatenate([high, low], axis=0), mode_refs[a][...], preferred_element_type=jnp.float32
            )
            right = right[:own] + right[own:]
            change = change + right[:, :mode_count] + right[:, mode_count:]
        coeffs = coeffs + TIME_STEP * (forcing - change)
    out_ref[...] = coeffs


def shards(modes, cell_weight, seeds, coeff_table, force_table, visc_table):
    components, mode_count, layers, across = modes.shape
    own = seeds.shape[0]
    lanes = layers * across
    devices = lax.axis_size("space")
    rows = select(seeds, coeff_table, force_table, visc_table)
    groups, by_offset = gather(modes, cell_weight, rows)
    me = jnp.full((1, 128), lax.axis_index("space") if by_offset else 0, jnp.int32)
    middle = center(groups[0][0][0], components)
    copies = 2 if 8 * components * devices * lanes * mode_count <= COPIES_LIMIT else 1
    shapes = state_of(copies, components, devices, own, lanes, mode_count)
    state = ()
    for group in groups[:-1]:
        state = absorb(copies, me, rows[0], middle, group, shapes, state)
    late = groups[-1]
    vmem = pl.BlockSpec(memory_space=pltpu.VMEM)
    operands = (me, *rows, middle, *(one[0] for one in late), *state)
    size = sum(operand.size * operand.dtype.itemsize for operand in (*operands, *shapes))
    out = jax.ShapeDtypeStruct((own, mode_count), jnp.float32)
    out, *_ = pl.pallas_call(
        functools.partial(step_kernel, [one[1:] for one in late], copies, across),
        out_shape=(out, *shapes),
        in_specs=[vmem] * len(operands),
        out_specs=(vmem,) * (1 + len(shapes)),
        input_output_aliases={len(operands) - len(state) + i: 1 + i for i in range(len(state))},
        compiler_params=pltpu.CompilerParams(vmem_limit_bytes=size + 4 * 1024 * 1024),
        name="steps",
    )(*operands)
    return out


def solution(mesh):
    placed = (
        P("groups", None, "space", None),
        P("space", "groups"),
        P(("groups", "space")),
        P(),
        P(),
        P(),
    )
    return jax.shard_map(
        shards, mesh=mesh, in_specs=placed, out_specs=P(("groups", "space"), None), check_vma=False
    )
```
